32 devices in a mesh: blk: 8 (over z, x), feat: 4 (over y, core).
Axes of the slice: x: 2, y: 2, z: 4, core: 2. Of those that a mesh axis runs over, the one named last changes fastest.
Arguments:
- points: bfloat16 [1024, 8192], P('blk', 'feat'), may hold values from -12 to 12
- centers: bfloat16 [128, 8192], P('blk', 'feat'), may hold values from -12 to 12
- coefs: bfloat16 [128, 1024], P('blk', 'feat'), may hold values from -16 to 16
Outputs:
- normal_prod: float32 [128, 1024], P('blk', 'feat')
The draws below stay inside these ranges and needn't reach their ends.
All inputs are finite; a program needn't handle non-finite values.
Results may differ from the reference program's by a relative error of at most 0.0011.
Values may be sent and summed in bfloat16 or wider, within the bound.
No kernel may reach another device: no remote copies, remote signals or barrier semaphores. Data moves between devices by JAX's collectives and lax.ppermute only.
A program may use at most 64 MiB of HBM per device.

```python
import math
import jax
import jax.numpy as jnp
from jax import lax

F = 8192
L = 1024
NPTS = 1024
M = 128


def field_law():
    return (16, 1.0, 2.0, 0.8, 0.97)


def mixed_rows(key, row_total, salt_id):
    latent_dims, latent_var, resid_var, mix_low, mix_high = field_law()
    basis_rows = jax.random.normal(jax.random.fold_in(key, 101), (latent_dims, F), jnp.float32)
    latent = jax.random.normal(jax.random.fold_in(key, salt_id), (row_total, latent_dims), jnp.float32)
    latent = latent * jnp.sqrt(latent_var / latent_dims)
    residual = jax.random.normal(jax.random.fold_in(key, salt_id + 1), (row_total, F), jnp.float32)
    residual = residual * jnp.sqrt(resid_var)
    return jnp.dot(latent, basis_rows, precision=lax.Precision.HIGHEST) + residual


def draw_centers(key, part):
    return jnp.clip(mixed_rows(key, M, 3), -12.0, 12.0).astype(jnp.bfloat16)


def draw_points(key, part):
    latent_dims, latent_var, resid_var, mix_low, mix_high = field_law()
    anchors = mixed_rows(key, M, 3)
    fresh_rows = mixed_rows(key, NPTS, 1)
    owner_row = jax.random.randint(jax.random.fold_in(key, 7), (NPTS,), 0, M)
    mix_weight = jax.random.uniform(jax.random.fold_in(key, 9), (NPTS, 1), jnp.float32, mix_low, mix_high)
    mixed = mix_weight * jnp.take(anchors, owner_row, axis=0) + jnp.sqrt(1.0 - mix_weight * mix_weight) * fresh_rows
    return jnp.clip(mixed, -12.0, 12.0).astype(jnp.bfloat16)


def levels(own_key, shape, pieces, low, largest):
    level = 1.0
    for axis_at, parts in pieces:
        heights = jax.random.uniform(jax.random.fold_in(jax.random.fold_in(own_key, 6), axis_at), (parts,), jnp.float32, low / len(pieces), largest / len(pieces))
        level = level * jnp.repeat(jnp.exp(heights), shape[axis_at] // parts).reshape((-1,) + (1,) * (len(shape) - 1 - axis_at))
    return level


def scatter_about(key, dims, spread, most, split=(), kind=jnp.bfloat16):
    result = spread * jax.random.normal(key, dims, jnp.float32)
    if split:
        result = result * levels(key, dims, split, -0.22, 0.18)
    return jnp.clip(result, -most, most).astype(kind)


def setup_inputs(seed: int = 0) -> dict:
    splits = jax.random.split(jax.random.key(seed), 4)
    points = draw_points(jax.random.fold_in(splits[3], 71), 0)
    centers = draw_centers(jax.random.fold_in(splits[3], 71), 0)
    coefs = scatter_about(splits[2], (M, L), 2.5, 16.0, ((0, 8), (1, 4)))
    return {"points": points, "centers": centers, "coefs": coefs}


def reference(points, centers, coefs):
    point_sq = jnp.einsum('nf,nf->n', points, points, preferred_element_type=jnp.float32)
    center_sq = jnp.einsum('mf,mf->m', centers, centers, preferred_element_type=jnp.float32)
    cross_dot = lax.dot_general(points, centers, (((1,), (1,)), ((), ())), preferred_element_type=jnp.float32)
    dist = point_sq[:, None] + center_sq[None, :] - 2.0 * cross_dot
    kernel = jnp.exp(-dist / F).astype(jnp.bfloat16)
    fitted = jnp.dot(kernel, coefs, preferred_element_type=jnp.float32).astype(jnp.bfloat16)
    summed = lax.dot_general(kernel, fitted, (((0,), (0,)), ((), ())), preferred_element_type=jnp.float32)
    return summed * (1.0 / math.sqrt(NPTS))
```

```python
import math

import jax
import jax.numpy as jnp
from jax import lax
from jax.experimental import pallas as pl
from jax.experimental.pallas import tpu as pltpu
from jax.sharding import PartitionSpec as P

BF16 = jnp.bfloat16
F32 = jnp.float32
LANES = 128
VMEM = pl.BlockSpec(memory_space=pltpu.VMEM)


def swap(x, axis, bits):
    n = lax.axis_size(axis)
    return lax.ppermute(x, axis, [(i, i ^ bits) for i in range(n)])


def call(kernel, outs, *args, scratch=()):
    return pl.pallas_call(
        kernel,
        out_shape=outs,
        in_specs=[VMEM] * len(args),
        out_specs=jax.tree.map(lambda _: VMEM, outs),
        scratch_shapes=list(scratch),
    )(*args)


def dist_kernel(order, points_ref, *refs):
    tiles, (mine_ref, other_ref, centers, part) = refs[: len(order)], refs[len(order) :]
    rows = tiles[0].shape[0]
    half = mine_ref.shape[0]
    blk = lax.axis_index("blk")
    for k, tile in zip(order, tiles):
        at = pl.multiple_of((blk ^ k) * rows, rows)
        centers[pl.ds(at, rows), :] = tile[...]
    points = points_ref[...]
    cross = lax.dot_general(
        centers[...], points, (((1,), (1,)), ((), ())), preferred_element_type=F32
    )
    wide = points.astype(F32)
    point_sq = jnp.sum((wide * wide).T, axis=0, keepdims=True)
    wide = centers[...].astype(F32)
    center_sq = jnp.sum(wide * wide, axis=1, keepdims=True)
    part[...] = point_sq + center_sq - 2.0 * cross
    core = lax.axis_index("feat") % 2
    mine_ref[...] = part[pl.ds(pl.multiple_of(core * half, half), half), :]
    other_ref[...] = part[pl.ds(pl.multiple_of((1 - core) * half, half), half), :]


def send_kernel(features, a_ref, b_ref, coefs_ref, out_ref):
    half = a_ref.shape[0]
    rows = coefs_ref.shape[0]
    out_ref[:half, :] = jnp.exp(-(a_ref[...] + b_ref[...]) / features).astype(BF16)
    for i in range(coefs_ref.shape[1] // LANES):
        at = half + i * rows
        out_ref[at : at + rows, :] = coefs_ref[:, i * LANES : (i + 1) * LANES]


def product_kernel(orders, rows, scale, *refs):
    n = len(orders)
    mine, other, (out_ref, kernel, coefs) = refs[:n], refs[n : 2 * n], refs[2 * n :]
    half = kernel.shape[0] // 2
    blk = lax.axis_index("blk")
    core = lax.axis_index("feat") % 2
    at_mine = pl.multiple_of(core * half, half)
    at_other = pl.multiple_of((1 - core) * half, half)
    lane = 0
    for order, m_ref, o_ref in zip(orders, mine, other):
        size = m_ref.shape[0] // len(order)
        for i, k in enumerate(order):
            lanes = slice(lane, lane + LANES)
            kernel[pl.ds(at_mine, half), lanes] = m_ref[i * size : i * size + half, :]
            kernel[pl.ds(at_other, half), lanes] = o_ref[i * size : i * size + half, :]
            at = pl.multiple_of((blk ^ k) * rows, rows)
            for j in range(coefs.shape[1] // LANES):
                top = i * size + half + j * rows
                coefs[pl.ds(at, rows), j * LANES : (j + 1) * LANES] = m_ref[top : top + rows, :]
            lane += LANES
    fitted = lax.dot_general(
        coefs[...].T, kernel[...], (((1,), (0,)), ((), ())), preferred_element_type=F32
    ).astype(BF16)
    own = kernel[pl.ds(pl.multiple_of(blk * rows, rows), rows), :]
    out_ref[...] = scale * lax.dot_general(
        own, fitted, (((1,), (1,)), ((), ())), preferred_element_type=F32
    )


def on_device(points, centers, coefs):
    blks = lax.axis_size("blk")
    rows, local_points = centers.shape[0], points.shape[0]
    features = points.shape[1] * lax.axis_size("feat")
    all_rows = rows * blks
    half = all_rows // 2
    line = [k for k in (4, 6, 2) if k < blks]

    tiles = {0: centers}
    for k in line:
        tiles[k] = swap(centers, "blk", k)
    for k in [0] + line:
        tiles[k ^ 1] = swap(tiles[k], "blk", 1)
    order = sorted(tiles)
    part = jax.ShapeDtypeStruct((half, local_points), F32)
    mine, other = call(
        lambda *r: dist_kernel(order, *r),
        (part, part),
        points,
        *[tiles[k] for k in order],
        scratch=[pltpu.VMEM((all_rows, points.shape[1]), BF16), pltpu.VMEM((all_rows, local_points), F32)],
    )
    mine = mine + swap(other, "feat", 1)
    far = swap(mine, "feat", 2)
    size = half + rows * (coefs.shape[1] // LANES)
    tile = call(
        lambda *r: send_kernel(float(features), *r),
        jax.ShapeDtypeStruct((size, local_points), BF16),
        mine,
        far,
        coefs,
    )
    column = jnp.concatenate([tile] + [swap(tile, "blk", k) for k in line], axis=0)
    across = swap(column, "blk", 1)
    orders = [[0] + line, [1] + [k ^ 1 for k in line]]
    scale = 1.0 / math.sqrt(local_points * blks)
    return call(
        lambda *r: product_kernel(orders, rows, scale, *r),
        jax.ShapeDtypeStruct((rows, coefs.shape[1]), F32),
        column,
        across,
        swap(column, "feat", 1),
        swap(across, "feat", 1),
        scratch=[pltpu.VMEM((all_rows, local_points * blks), BF16), pltpu.VMEM((all_rows, coefs.shape[1]), BF16)],
    )


def on_device_large(points, centers, coefs):
    features = points.shape[1] * lax.axis_size("feat")
    point_sq = jnp.einsum("nf,nf->n", points, points, preferred_element_type=F32)
    center_piece = lax.all_gather(centers, "blk", axis=0, tiled=True)
    center_sq = jnp.einsum("mf,mf->m", center_piece, center_piece, preferred_element_type=F32)
    cross_dot = lax.dot_general(
        points, center_piece, (((1,), (1,)), ((), ())), preferred_element_type=F32
    )
    dist_tile = point_sq[:, None] + center_sq[None, :] - 2.0 * cross_dot
    all_coefs = lax.all_gather(coefs, "blk", axis=0, tiled=True)
    dist = lax.psum(dist_tile, "feat")
    kernel = jnp.exp(-dist / features).astype(BF16)
    fitted = jnp.dot(kernel, all_coefs, preferred_element_type=F32).astype(BF16)
    summed = lax.psum_scatter(
        lax.dot_general(kernel, fitted, (((0,), (0,)), ((), ())), preferred_element_type=F32),
        "blk",
        scatter_dimension=0,
        tiled=True,
    )
    return summed * (1.0 / math.sqrt(points.shape[0] * lax.axis_size("blk")))


def solution(mesh):
    small = mesh.shape["blk"] == 8 and mesh.shape["feat"] == 4
    in_specs = (P("blk", "feat"), P("blk", "feat"), P("blk", "feat"))
    return jax.shard_map(
        on_device if small else on_device_large,
        mesh=mesh,
        in_specs=in_specs,
        out_specs=P("blk", "feat"),
        check_vma=False,
    )
```

```python
import math

import jax
import jax.numpy as jnp
from jax import lax
from jax.experimental import pallas as pl
from jax.experimental.pallas import tpu as pltpu
from jax.sharding import PartitionSpec as P

BF16 = jnp.bfloat16
F32 = jnp.float32
LANES = 128
VMEM = pl.BlockSpec(memory_space=pltpu.VMEM)


def swap(x, axis, bits):
    n = lax.axis_size(axis)
    return lax.ppermute(x, axis, [(i, i ^ bits) for i in range(n)])


def near(x):
    return pltpu.with_memory_space_constraint(x, pltpu.VMEM)


def call(kernel, outs, *args, scratch=()):
    return pl.pallas_call(
        kernel,
        out_shape=[pltpu.VMEM(o.shape, o.dtype) for o in outs],
        in_specs=[VMEM] * len(args),
        out_specs=[VMEM] * len(outs),
        scratch_shapes=list(scratch),
    )(*[near(x) for x in args])


def dist_kernel(order, points_ref, *refs):
    tiles, (mine_ref, other_ref, centers, part) = refs[: len(order)], refs[len(order) :]
    rows = tiles[0].shape[0]
    half = mine_ref.shape[0]
    blk = lax.axis_index("blk")
    for k, tile in zip(order, tiles):
        at = pl.multiple_of((blk ^ k) * rows, rows)
        centers[pl.ds(at, rows), :] = tile[...]
    points = points_ref[...]
    cross = lax.dot_general(
        centers[...], points, (((1,), (1,)), ((), ())), preferred_element_type=F32
    )
    wide = points.astype(F32)
    point_sq = jnp.sum((wide * wide).T, axis=0, keepdims=True)
    wide = centers[...].astype(F32)
    center_sq = jnp.sum(wide * wide, axis=1, keepdims=True)
    part[...] = point_sq + center_sq - 2.0 * cross
    core = lax.axis_index("feat") % 2
    mine_ref[...] = part[pl.ds(pl.multiple_of(core * half, half), half), :]
    other_ref[...] = part[pl.ds(pl.multiple_of((1 - core) * half, half), half), :]


def send_kernel(features, a_ref, b_ref, coefs_ref, out_ref):
    half = a_ref.shape[0]
    rows = coefs_ref.shape[0]
    out_ref[:half, :] = jnp.exp(-(a_ref[...] + b_ref[...]) / features).astype(BF16)
    for i in range(coefs_ref.shape[1] // LANES):
        at = half + i * rows
        out_ref[at : at + rows, :] = coefs_ref[:, i * LANES : (i + 1) * LANES]


def product_kernel(orders, rows, scale, *refs):
    n = len(orders)
    mine, other, (out_ref, kernel, coefs) = refs[:n], refs[n : 2 * n], refs[2 * n :]
    half = kernel.shape[0] // 2
    blk = lax.axis_index("blk")
    core = lax.axis_index("feat") % 2
    at_mine = pl.multiple_of(core * half, half)
    at_other = pl.multiple_of((1 - core) * half, half)
    lane = 0
    for order, m_ref, o_ref in zip(orders, mine, other):
        size = m_ref.shape[0] // len(order)
        for i, k in enumerate(order):
            lanes = slice(lane, lane + LANES)
            kernel[pl.ds(at_mine, half), lanes] = m_ref[i * size : i * size + half, :]
            kernel[pl.ds(at_other, half), lanes] = o_ref[i * size : i * size + half, :]
            at = pl.multiple_of((blk ^ k) * rows, rows)
            for j in range(coefs.shape[1] // LANES):
                top = i * size + half + j * rows
                coefs[pl.ds(at, rows), j * LANES : (j + 1) * LANES] = m_ref[top : top + rows, :]
            lane += LANES
    fitted = lax.dot_general(
        coefs[...].T, kernel[...], (((1,), (0,)), ((), ())), preferred_element_type=F32
    ).astype(BF16)
    own = kernel[pl.ds(pl.multiple_of(blk * rows, rows), rows), :]
    out_ref[...] = scale * lax.dot_general(
        own, fitted, (((1,), (1,)), ((), ())), preferred_element_type=F32
    )


def on_device(points, centers, coefs):
    blks = lax.axis_size("blk")
    rows, local_points = centers.shape[0], points.shape[0]
    features = points.shape[1] * lax.axis_size("feat")
    all_rows = rows * blks
    half = all_rows // 2
    line = [k for k in (4, 6, 2) if k < blks]

    tiles = {0: centers}
    for k in line:
        tiles[k] = swap(centers, "blk", k)
    for k in [0] + line:
        tiles[k ^ 1] = swap(tiles[k], "blk", 1)
    order = sorted(tiles)
    part = jax.ShapeDtypeStruct((half, local_points), F32)
    mine, other = call(
        lambda *r: dist_kernel(order, *r),
        [part, part],
        points,
        *[tiles[k] for k in order],
        scratch=[pltpu.VMEM((all_rows, points.shape[1]), BF16), pltpu.VMEM((all_rows, local_points), F32)],
    )
    mine = mine + swap(other, "feat", 1)
    far = swap(mine, "feat", 2)
    size = half + rows * (coefs.shape[1] // LANES)
    (tile,) = call(
        lambda *r: send_kernel(float(features), *r),
        [jax.ShapeDtypeStruct((size, local_points), BF16)],
        mine,
        far,
        coefs,
    )
    column = jnp.concatenate([tile] + [swap(tile, "blk", k) for k in line], axis=0)
    across = swap(column, "blk", 1)
    orders = [[0] + line, [1] + [k ^ 1 for k in line]]
    scale = 1.0 / math.sqrt(local_points * blks)
    (out,) = call(
        lambda *r: product_kernel(orders, rows, scale, *r),
        [jax.ShapeDtypeStruct((rows, coefs.shape[1]), F32)],
        column,
        across,
        swap(column, "feat", 1),
        swap(across, "feat", 1),
        scratch=[pltpu.VMEM((all_rows, local_points * blks), BF16), pltpu.VMEM((all_rows, coefs.shape[1]), BF16)],
    )
    return out


def on_device_large(points, centers, coefs):
    features = points.shape[1] * lax.axis_size("feat")
    point_sq = jnp.einsum("nf,nf->n", points, points, preferred_element_type=F32)
    center_piece = lax.all_gather(centers, "blk", axis=0, tiled=True)
    center_sq = jnp.einsum("mf,mf->m", center_piece, center_piece, preferred_element_type=F32)
    cross_dot = lax.dot_general(
        points, center_piece, (((1,), (1,)), ((), ())), preferred_element_type=F32
    )
    dist_tile = point_sq[:, None] + center_sq[None, :] - 2.0 * cross_dot
    all_coefs = lax.all_gather(coefs, "blk", axis=0, tiled=True)
    dist = lax.psum(dist_tile, "feat")
    kernel = jnp.exp(-dist / features).astype(BF16)
    fitted = jnp.dot(kernel, all_coefs, preferred_element_type=F32).astype(BF16)
    summed = lax.psum_scatter(
        lax.dot_general(kernel, fitted, (((0,), (0,)), ((), ())), preferred_element_type=F32),
        "blk",
        scatter_dimension=0,
        tiled=True,
    )
    return summed * (1.0 / math.sqrt(points.shape[0] * lax.axis_size("blk")))


def solution(mesh):
    small = mesh.shape["blk"] == 8 and mesh.shape["feat"] == 4
    in_specs = (P("blk", "feat"), P("blk", "feat"), P("blk", "feat"))
    return jax.shard_map(
        on_device if small else on_device_large,
        mesh=mesh,
        in_specs=in_specs,
        out_specs=P("blk", "feat"),
        check_vma=False,
    )
```

```python
import math

import jax
import jax.numpy as jnp
from jax import lax
from jax.experimental import pallas as pl
from jax.experimental.pallas import tpu as pltpu
from jax.sharding import PartitionSpec as P

BF16 = jnp.bfloat16
F32 = jnp.float32
LANES = 128
VMEM = pl.BlockSpec(memory_space=pltpu.VMEM)


def swap(x, axis, bits):
    n = lax.axis_size(axis)
    return lax.ppermute(x, axis, [(i, i ^ bits) for i in range(n)])


def near(x):
    return pltpu.with_memory_space_constraint(x, pltpu.VMEM)


def call(kernel, outs, *args, scratch=()):
    return pl.pallas_call(
        kernel,
        out_shape=[pltpu.VMEM(o.shape, o.dtype) for o in outs],
        in_specs=[VMEM] * len(args),
        out_specs=[VMEM] * len(outs),
        scratch_shapes=list(scratch),
    )(*[near(x) for x in args])


def prepare_kernel(points_ref, centers_ref, points_out, centers_out, square_out):
    points_out[...] = points_ref[...]
    centers_out[...] = centers_ref[...]
    wide = points_ref[...].astype(F32)
    square_out[...] = jnp.sum((wide * wide).T, axis=0, keepdims=True)


def dist_kernel(order, points_ref, square_ref, *refs):
    tiles, (part_ref, centers) = refs[: len(order)], refs[len(order) :]
    rows = tiles[0].shape[0]
    blk = lax.axis_index("blk")
    for k, tile in zip(order, tiles):
        at = pl.multiple_of((blk ^ k) * rows, rows)
        centers[pl.ds(at, rows), :] = tile[...]
    cross = lax.dot_general(
        centers[...], points_ref[...], (((1,), (1,)), ((), ())), preferred_element_type=F32
    )
    wide = centers[...].astype(F32)
    center_sq = jnp.sum(wide * wide, axis=1, keepdims=True)
    part_ref[...] = square_ref[...] + center_sq - 2.0 * cross


def send_kernel(features, a_ref, b_ref, coefs_ref, others_ref, out_ref):
    all_rows, rows = a_ref.shape[0], coefs_ref.shape[0]
    out_ref[:all_rows, :] = jnp.exp(-(a_ref[...] + b_ref[...]) / features).astype(BF16)
    core = lax.axis_index("feat") % 2
    pieces = coefs_ref.shape[1] // LANES
    for half, ref in ((core, coefs_ref), (1 - core, others_ref)):
        for i in range(pieces):
            at = pl.multiple_of(all_rows + (half * pieces + i) * rows, rows)
            out_ref[pl.ds(at, rows), :] = ref[:, i * LANES : (i + 1) * LANES]


def product_kernel(mine_order, other_order, rows, scale, *refs):
    n, m = len(mine_order[0]), len(other_order[0])
    tiles, (out_ref, kernel, coefs) = refs[: n + m], refs[n + m :]
    all_rows = kernel.shape[0]
    blk = lax.axis_index("blk")
    core = lax.axis_index("feat") % 2
    pieces = coefs.shape[1] // LANES
    for i, tile in enumerate(tiles):
        a, b = (mine_order[0][i], mine_order[1][i]) if i < n else (other_order[0][i - n], other_order[1][i - n])
        kernel[:, i * LANES : (i + 1) * LANES] = tile[:all_rows, :]
        at = pl.multiple_of((blk ^ jnp.where(core == 0, a, b)) * rows, rows)
        for j in range(pieces):
            top = pl.multiple_of(all_rows + (core * pieces + j) * rows, rows)
            coefs[pl.ds(at, rows), j * LANES : (j + 1) * LANES] = tile[pl.ds(top, rows), :]
    fitted = lax.dot_general(
        coefs[...].T, kernel[...], (((1,), (0,)), ((), ())), preferred_element_type=F32
    ).astype(BF16)
    own = kernel[pl.ds(pl.multiple_of(blk * rows, rows), rows), :]
    out_ref[...] = scale * lax.dot_general(
        own, fitted, (((1,), (1,)), ((), ())), preferred_element_type=F32
    )


def swap_by_core(x, even, odd):
    feats, blks = lax.axis_size("feat"), lax.axis_size("blk")
    pairs = [
        (b * feats + f, (b ^ (odd if f % 2 else even)) * feats + f)
        for b in range(blks)
        for f in range(feats)
    ]
    return lax.ppermute(x, ("blk", "feat"), pairs)


def on_device(points, centers, coefs):
    blks = lax.axis_size("blk")
    rows, local_points = centers.shape[0], points.shape[0]
    features = points.shape[1] * lax.axis_size("feat")
    all_rows = rows * blks
    line = [k for k in (4, 6, 2) if k < blks]

    tiles = {}
    for k in line:
        tiles[k] = swap(centers, "blk", k)
    tiles[1] = swap(centers, "blk", 1)
    for k in line:
        tiles[k ^ 1] = swap(tiles[k], "blk", 1)
    points, tiles[0], square = pl.pallas_call(
        prepare_kernel,
        out_shape=[pltpu.VMEM(points.shape, BF16), pltpu.VMEM(centers.shape, BF16), pltpu.VMEM((1, local_points), F32)],
        in_specs=[VMEM] * 2,
        out_specs=[VMEM] * 3,
        cost_estimate=pl.CostEstimate(flops=2 * points.size, bytes_accessed=2 * points.size, transcendentals=0),
    )(points, centers)
    others = swap(coefs, "feat", 1)
    order = sorted(tiles)
    (part,) = call(
        lambda *r: dist_kernel(order, *r),
        [jax.ShapeDtypeStruct((all_rows, local_points), F32)],
        points,
        square,
        *[tiles[k] for k in order],
        scratch=[pltpu.VMEM((all_rows, points.shape[1]), BF16)],
    )
    part = part + swap(part, "feat", 1)
    far = swap(part, "feat", 2)
    pieces = coefs.shape[1] // LANES
    (tile,) = call(
        lambda *r: send_kernel(float(features), *r),
        [jax.ShapeDtypeStruct((all_rows + 2 * pieces * rows, local_points), BF16)],
        part,
        far,
        coefs,
        others,
    )
    mine_order = ([0, 4, 5, 3, 2], [0, 6, 7, 1, 2])
    mine = [tile] + [swap_by_core(tile, a, b) for a, b in list(zip(*mine_order))[1:]]
    other_order = (mine_order[1][1:-1], mine_order[0][1:-1])
    other = [swap(x, "feat", 1) for x in mine[1:-1]]
    scale = 1.0 / math.sqrt(local_points * blks)
    (out,) = call(
        lambda *r: product_kernel(mine_order, other_order, rows, scale, *r),
        [jax.ShapeDtypeStruct((rows, coefs.shape[1]), F32)],
        *mine,
        *other,
        scratch=[pltpu.VMEM((all_rows, local_points * blks), BF16), pltpu.VMEM((all_rows, coefs.shape[1]), BF16)],
    )
    return out


def on_device_large(points, centers, coefs):
    features = points.shape[1] * lax.axis_size("feat")
    point_sq = jnp.einsum("nf,nf->n", points, points, preferred_element_type=F32)
    center_piece = lax.all_gather(centers, "blk", axis=0, tiled=True)
    center_sq = jnp.einsum("mf,mf->m", center_piece, center_piece, preferred_element_type=F32)
    cross_dot = lax.dot_general(
        points, center_piece, (((1,), (1,)), ((), ())), preferred_element_type=F32
    )
    dist_tile = point_sq[:, None] + center_sq[None, :] - 2.0 * cross_dot
    all_coefs = lax.all_gather(coefs, "blk", axis=0, tiled=True)
    dist = lax.psum(dist_tile, "feat")
    kernel = jnp.exp(-dist / features).astype(BF16)
    fitted = jnp.dot(kernel, all_coefs, preferred_element_type=F32).astype(BF16)
    summed = lax.psum_scatter(
        lax.dot_general(kernel, fitted, (((0,), (0,)), ((), ())), preferred_element_type=F32),
        "blk",
        scatter_dimension=0,
        tiled=True,
    )
    return summed * (1.0 / math.sqrt(points.shape[0] * lax.axis_size("blk")))


def solution(mesh):
    small = mesh.shape["blk"] == 8 and mesh.shape["feat"] == 4
    in_specs = (P("blk", "feat"), P("blk", "feat"), P("blk", "feat"))
    return jax.shard_map(
        on_device if small else on_device_large,
        mesh=mesh,
        in_specs=in_specs,
        out_specs=P("blk", "feat"),
        check_vma=False,
    )
```

```python
import math

import jax
import jax.numpy as jnp
from jax import lax
from jax.experimental import pallas as pl
from jax.experimental.pallas import tpu as pltpu
from jax.sharding import PartitionSpec as P

BF16 = jnp.bfloat16
F32 = jnp.float32
GATHER = ((0, 1), (0, 4), (1, 4), (0, 2), (1, 2), (0, 6), (6, 1))
SPREAD = ((0, 6, 7), (0, 4, 5), (0, 2, 3), (0, 1, 1))
LANES = 128
VMEM = pl.BlockSpec(memory_space=pltpu.VMEM)


def swap(x, axis, bits):
    n = lax.axis_size(axis)
    return lax.ppermute(x, axis, [(i, i ^ bits) for i in range(n)])


def near(x):
    return pltpu.with_memory_space_constraint(x, pltpu.VMEM)


def call(kernel, outs, *args, scratch=()):
    return pl.pallas_call(
        kernel,
        out_shape=[pltpu.VMEM(o.shape, o.dtype) for o in outs],
        in_specs=[VMEM] * len(args),
        out_specs=[VMEM] * len(outs),
        scratch_shapes=list(scratch),
    )(*[near(x) for x in args])


def prepare_kernel(points_ref, centers_ref, points_out, centers_out, square_out):
    points_out[...] = points_ref[...]
    centers_out[...] = centers_ref[...]
    wide = points_ref[...].astype(F32)
    square_out[...] = jnp.sum((wide * wide).T, axis=0, keepdims=True)


def dist_kernel(order, points_ref, square_ref, *refs):
    tiles, (part_ref, centers) = refs[: len(order)], refs[len(order) :]
    rows = tiles[0].shape[0]
    blk = lax.axis_index("blk")
    for k, tile in zip(order, tiles):
        at = pl.multiple_of((blk ^ k) * rows, rows)
        centers[pl.ds(at, rows), :] = tile[...]
    cross = lax.dot_general(
        centers[...], points_ref[...], (((1,), (1,)), ((), ())), preferred_element_type=F32
    )
    wide = centers[...].astype(F32)
    center_sq = jnp.sum(wide * wide, axis=1, keepdims=True)
    part_ref[...] = square_ref[...] + center_sq - 2.0 * cross


def send_kernel(features, a_ref, b_ref, coefs_ref, others_ref, out_ref):
    all_rows, rows = a_ref.shape[0], coefs_ref.shape[0]
    out_ref[:all_rows, :] = jnp.exp(-(a_ref[...] + b_ref[...]) / features).astype(BF16)
    core = lax.axis_index("feat") % 2
    pieces = coefs_ref.shape[1] // LANES
    for half, ref in ((core, coefs_ref), (1 - core, others_ref)):
        for i in range(pieces):
            at = pl.multiple_of(all_rows + (half * pieces + i) * rows, rows)
            out_ref[pl.ds(at, rows), :] = ref[:, i * LANES : (i + 1) * LANES]


def product_kernel(sources, rows, scale, *refs):
    tiles, (out_ref, kernel, coefs) = refs[: len(sources)], refs[len(sources) :]
    all_rows = kernel.shape[0]
    blk = lax.axis_index("blk")
    core = lax.axis_index("feat") % 2
    pieces = coefs.shape[1] // LANES
    for i, (tile, (even, odd)) in enumerate(zip(tiles, sources)):
        kernel[:, i * LANES : (i + 1) * LANES] = tile[:all_rows, :]
        at = pl.multiple_of((blk ^ jnp.where(core == 0, even, odd)) * rows, rows)
        for j in range(pieces):
            top = pl.multiple_of(all_rows + (core * pieces + j) * rows, rows)
            coefs[pl.ds(at, rows), j * LANES : (j + 1) * LANES] = tile[pl.ds(top, rows), :]
    fitted = lax.dot_general(
        coefs[...].T, kernel[...], (((1,), (0,)), ((), ())), preferred_element_type=F32
    ).astype(BF16)
    own = kernel[pl.ds(pl.multiple_of(blk * rows, rows), rows), :]
    out_ref[...] = scale * lax.dot_general(
        own, fitted, (((1,), (1,)), ((), ())), preferred_element_type=F32
    )


def swap_by_core(x, even, odd):
    feats, blks = lax.axis_size("feat"), lax.axis_size("blk")
    pairs = [
        (b * feats + f, (b ^ (odd if f % 2 else even)) * feats + f)
        for b in range(blks)
        for f in range(feats)
    ]
    return lax.ppermute(x, ("blk", "feat"), pairs)


def on_device(points, centers, coefs):
    blks = lax.axis_size("blk")
    rows, local_points = centers.shape[0], points.shape[0]
    features = points.shape[1] * lax.axis_size("feat")
    all_rows = rows * blks
    tiles = {0: centers}
    for held, bits in GATHER:
        tiles[held ^ bits] = swap(tiles[held], "blk", bits)
    points, tiles[0], square = pl.pallas_call(
        prepare_kernel,
        out_shape=[pltpu.VMEM(points.shape, BF16), pltpu.VMEM(centers.shape, BF16), pltpu.VMEM((1, local_points), F32)],
        in_specs=[VMEM] * 2,
        out_specs=[VMEM] * 3,
        cost_estimate=pl.CostEstimate(flops=2 * points.size, bytes_accessed=2 * points.size, transcendentals=0),
    )(points, centers)
    others = swap(coefs, "feat", 1)
    order = sorted(tiles)
    (part,) = call(
        lambda *r: dist_kernel(order, *r),
        [jax.ShapeDtypeStruct((all_rows, local_points), F32)],
        points,
        square,
        *[tiles[k] for k in order],
        scratch=[pltpu.VMEM((all_rows, points.shape[1]), BF16)],
    )
    part = part + swap(part, "feat", 1)
    far = swap(part, "feat", 2)
    pieces = coefs.shape[1] // LANES
    (tile,) = call(
        lambda *r: send_kernel(float(features), *r),
        [jax.ShapeDtypeStruct((all_rows + 2 * pieces * rows, local_points), BF16)],
        part,
        far,
        coefs,
        others,
    )
    held, sources = [tile], [(0, 0)]
    for at, even, odd in SPREAD:
        held.append(swap_by_core(held[at], even, odd))
        sources.append((sources[at][0] ^ even, sources[at][1] ^ odd))
    passed = [i for i, (even, odd) in enumerate(sources) if even != odd]
    held += [swap(held[i], "feat", 1) for i in passed]
    sources += [sources[i][::-1] for i in passed]
    scale = 1.0 / math.sqrt(local_points * blks)
    (out,) = call(
        lambda *r: product_kernel(sources, rows, scale, *r),
        [jax.ShapeDtypeStruct((rows, coefs.shape[1]), F32)],
        *held,
        scratch=[pltpu.VMEM((all_rows, local_points * blks), BF16), pltpu.VMEM((all_rows, coefs.shape[1]), BF16)],
    )
    return out


def on_device_large(points, centers, coefs):
    features = points.shape[1] * lax.axis_size("feat")
    point_sq = jnp.einsum("nf,nf->n", points, points, preferred_element_type=F32)
    center_piece = lax.all_gather(centers, "blk", axis=0, tiled=True)
    center_sq = jnp.einsum("mf,mf->m", center_piece, center_piece, preferred_element_type=F32)
    cross_dot = lax.dot_general(
        points, center_piece, (((1,), (1,)), ((), ())), preferred_element_type=F32
    )
    dist_tile = point_sq[:, None] + center_sq[None, :] - 2.0 * cross_dot
    all_coefs = lax.all_gather(coefs, "blk", axis=0, tiled=True)
    dist = lax.psum(dist_tile, "feat")
    kernel = jnp.exp(-dist / features).astype(BF16)
    fitted = jnp.dot(kernel, all_coefs, preferred_element_type=F32).astype(BF16)
    summed = lax.psum_scatter(
        lax.dot_general(kernel, fitted, (((0,), (0,)), ((), ())), preferred_element_type=F32),
        "blk",
        scatter_dimension=0,
        tiled=True,
    )
    return summed * (1.0 / math.sqrt(points.shape[0] * lax.axis_size("blk")))


def solution(mesh):
    small = mesh.shape["blk"] == 8 and mesh.shape["feat"] == 4
    in_specs = (P("blk", "feat"), P("blk", "feat"), P("blk", "feat"))
    return jax.shard_map(
        on_device if small else on_device_large,
        mesh=mesh,
        in_specs=in_specs,
        out_specs=P("blk", "feat"),
        check_vma=False,
    )
```

```python
import math

import jax
import jax.numpy as jnp
from jax import lax
from jax.experimental import pallas as pl
from jax.experimental.pallas import tpu as pltpu
from jax.sharding import PartitionSpec as P

BF16 = jnp.bfloat16
F32 = jnp.float32
GATHER = ((0, 2, 5), (0, 1, 2), (0, 4, 1), (2, 2, 1), (0, 6, 6), (2, 4, 6), (5, 1, 1))
SPREAD = ((0, 4, 5), (0, 6, 7), (0, 2, 3), (0, 1, 1))
LANES = 128
VMEM = pl.BlockSpec(memory_space=pltpu.VMEM)


def swap(x, axis, bits):
    n = lax.axis_size(axis)
    return lax.ppermute(x, axis, [(i, i ^ bits) for i in range(n)])


def near(x):
    return pltpu.with_memory_space_constraint(x, pltpu.VMEM)


def call(kernel, outs, *args, scratch=()):
    return pl.pallas_call(
        kernel,
        out_shape=[pltpu.VMEM(o.shape, o.dtype) for o in outs],
        in_specs=[VMEM] * len(args),
        out_specs=[VMEM] * len(outs),
        scratch_shapes=list(scratch),
    )(*[near(x) for x in args])


def prepare_kernel(points_ref, centers_ref, points_out, centers_out, square_out):
    points_out[...] = points_ref[...]
    centers_out[...] = centers_ref[...]
    wide = points_ref[...].astype(F32)
    square_out[...] = jnp.sum((wide * wide).T, axis=0, keepdims=True)


def dist_kernel(sources, points_ref, square_ref, *refs):
    tiles, (part_ref, centers) = refs[: len(sources)], refs[len(sources) :]
    rows = tiles[0].shape[0]
    blk = lax.axis_index("blk")
    core = lax.axis_index("feat") % 2
    for (even, odd), tile in zip(sources, tiles):
        at = pl.multiple_of((blk ^ jnp.where(core == 0, even, odd)) * rows, rows)
        centers[pl.ds(at, rows), :] = tile[...]
    cross = lax.dot_general(
        centers[...], points_ref[...], (((1,), (1,)), ((), ())), preferred_element_type=F32
    )
    wide = centers[...].astype(F32)
    center_sq = jnp.sum(wide * wide, axis=1, keepdims=True)
    part_ref[...] = square_ref[...] + center_sq - 2.0 * cross


def send_kernel(features, a_ref, b_ref, coefs_ref, others_ref, out_ref):
    all_rows, rows = a_ref.shape[0], coefs_ref.shape[0]
    out_ref[:all_rows, :] = jnp.exp(-(a_ref[...] + b_ref[...]) / features).astype(BF16)
    core = lax.axis_index("feat") % 2
    pieces = coefs_ref.shape[1] // LANES
    for half, ref in ((core, coefs_ref), (1 - core, others_ref)):
        for i in range(pieces):
            at = pl.multiple_of(all_rows + (half * pieces + i) * rows, rows)
            out_ref[pl.ds(at, rows), :] = ref[:, i * LANES : (i + 1) * LANES]


def product_kernel(sources, rows, scale, *refs):
    tiles, (out_ref, kernel, coefs) = refs[: len(sources)], refs[len(sources) :]
    all_rows = kernel.shape[0]
    blk = lax.axis_index("blk")
    core = lax.axis_index("feat") % 2
    pieces = coefs.shape[1] // LANES
    for i, (tile, (even, odd)) in enumerate(zip(tiles, sources)):
        kernel[:, i * LANES : (i + 1) * LANES] = tile[:all_rows, :]
        at = pl.multiple_of((blk ^ jnp.where(core == 0, even, odd)) * rows, rows)
        for j in range(pieces):
            top = pl.multiple_of(all_rows + (core * pieces + j) * rows, rows)
            coefs[pl.ds(at, rows), j * LANES : (j + 1) * LANES] = tile[pl.ds(top, rows), :]
    fitted = lax.dot_general(
        coefs[...].T, kernel[...], (((1,), (0,)), ((), ())), preferred_element_type=F32
    ).astype(BF16)
    own = kernel[pl.ds(pl.multiple_of(blk * rows, rows), rows), :]
    out_ref[...] = scale * lax.dot_general(
        own, fitted, (((1,), (1,)), ((), ())), preferred_element_type=F32
    )


def swap_by_core(x, even, odd):
    feats, blks = lax.axis_size("feat"), lax.axis_size("blk")
    pairs = [
        (b * feats + f, (b ^ (odd if f % 2 else even)) * feats + f)
        for b in range(blks)
        for f in range(feats)
    ]
    return lax.ppermute(x, ("blk", "feat"), pairs)


def gather(x, steps):
    held, sources = [x], [(0, 0)]
    for at, even, odd in steps:
        held.append(swap_by_core(held[at], even, odd))
        sources.append((sources[at][0] ^ even, sources[at][1] ^ odd))
    return held, sources


def on_device(points, centers, coefs):
    blks = lax.axis_size("blk")
    rows, local_points = centers.shape[0], points.shape[0]
    features = points.shape[1] * lax.axis_size("feat")
    all_rows = rows * blks
    tiles, sources = gather(centers, GATHER)
    points, tiles[0], square = pl.pallas_call(
        prepare_kernel,
        out_shape=[pltpu.VMEM(points.shape, BF16), pltpu.VMEM(centers.shape, BF16), pltpu.VMEM((1, local_points), F32)],
        in_specs=[VMEM] * 2,
        out_specs=[VMEM] * 3,
        cost_estimate=pl.CostEstimate(flops=2 * points.size, bytes_accessed=2 * points.size, transcendentals=0),
    )(points, centers)
    others = swap(coefs, "feat", 1)
    (part,) = call(
        lambda *r: dist_kernel(sources, *r),
        [jax.ShapeDtypeStruct((all_rows, local_points), F32)],
        points,
        square,
        *tiles,
        scratch=[pltpu.VMEM((all_rows, points.shape[1]), BF16)],
    )
    part = part + swap(part, "feat", 1)
    far = swap(part, "feat", 2)
    pieces = coefs.shape[1] // LANES
    (tile,) = call(
        lambda *r: send_kernel(float(features), *r),
        [jax.ShapeDtypeStruct((all_rows + 2 * pieces * rows, local_points), BF16)],
        part,
        far,
        coefs,
        others,
    )
    held, sources = gather(tile, SPREAD)
    passed = [i for i, (even, odd) in enumerate(sources) if even != odd]
    held += [swap(held[i], "feat", 1) for i in passed]
    sources += [sources[i][::-1] for i in passed]
    scale = 1.0 / math.sqrt(local_points * blks)
    (out,) = call(
        lambda *r: product_kernel(sources, rows, scale, *r),
        [jax.ShapeDtypeStruct((rows, coefs.shape[1]), F32)],
        *held,
        scratch=[pltpu.VMEM((all_rows, local_points * blks), BF16), pltpu.VMEM((all_rows, coefs.shape[1]), BF16)],
    )
    return out


def on_device_large(points, centers, coefs):
    features = points.shape[1] * lax.axis_size("feat")
    point_sq = jnp.einsum("nf,nf->n", points, points, preferred_element_type=F32)
    center_piece = lax.all_gather(centers, "blk", axis=0, tiled=True)
    center_sq = jnp.einsum("mf,mf->m", center_piece, center_piece, preferred_element_type=F32)
    cross_dot = lax.dot_general(
        points, center_piece, (((1,), (1,)), ((), ())), preferred_element_type=F32
    )
    dist_tile = point_sq[:, None] + center_sq[None, :] - 2.0 * cross_dot
    all_coefs = lax.all_gather(coefs, "blk", axis=0, tiled=True)
    dist = lax.psum(dist_tile, "feat")
    kernel = jnp.exp(-dist / features).astype(BF16)
    fitted = jnp.dot(kernel, all_coefs, preferred_element_type=F32).astype(BF16)
    summed = lax.psum_scatter(
        lax.dot_general(kernel, fitted, (((0,), (0,)), ((), ())), preferred_element_type=F32),
        "blk",
        scatter_dimension=0,
        tiled=True,
    )
    return summed * (1.0 / math.sqrt(points.shape[0] * lax.axis_size("blk")))


def solution(mesh):
    small = mesh.shape["blk"] == 8 and mesh.shape["feat"] == 4
    in_specs = (P("blk", "feat"), P("blk", "feat"), P("blk", "feat"))
    return jax.shard_map(
        on_device if small else on_device_large,
        mesh=mesh,
        in_specs=in_specs,
        out_specs=P("blk", "feat"),
        check_vma=False,
    )
```

```python
import math

import jax
import jax.numpy as jnp
from jax import lax
from jax.experimental import pallas as pl
from jax.experimental.pallas import tpu as pltpu
from jax.sharding import PartitionSpec as P

BF16 = jnp.bfloat16
F32 = jnp.float32
VMEM = pl.BlockSpec(memory_space=pltpu.VMEM)

GATHER = ((0, 2, 5), (0, 1, 2), (0, 4, 1), (2, 2, 1), (0, 6, 6), (2, 4, 6), (5, 1, 1))
SPREAD = ((0, 4, 5), (0, 6, 7), (0, 2, 3), (0, 1, 1))


def near(x):
    return pltpu.with_memory_space_constraint(x, pltpu.VMEM)


def call(kernel, outs, *args, scratch=()):
    return pl.pallas_call(
        kernel,
        out_shape=[pltpu.VMEM(*o) for o in outs],
        in_specs=[VMEM] * len(args),
        out_specs=[VMEM] * len(outs),
        scratch_shapes=list(scratch),
    )(*[near(x) for x in args])


def place(bits, rows):
    even, odd = bits
    core = lax.axis_index("feat") % 2
    return pl.multiple_of((lax.axis_index("blk") ^ jnp.where(core == 0, even, odd)) * rows, rows)


def prepare_kernel(points_ref, centers_ref, points_out, centers_out, square_out):
    points_out[...] = points_ref[...]
    centers_out[...] = centers_ref[...]
    wide = points_ref[...].astype(F32)
    square_out[...] = jnp.sum((wide * wide).T, axis=0, keepdims=True)


def dist_kernel(sources, points_ref, square_ref, *refs):
    tiles, (part_ref, centers) = refs[: len(sources)], refs[len(sources) :]
    rows = tiles[0].shape[0]
    for bits, tile in zip(sources, tiles):
        centers[pl.ds(place(bits, rows), rows), :] = tile[...]
    cross = lax.dot_general(
        centers[...], points_ref[...], (((1,), (1,)), ((), ())), preferred_element_type=F32
    )
    wide = centers[...].astype(F32)
    center_sq = jnp.sum(wide * wide, axis=1, keepdims=True)
    part_ref[...] = square_ref[...] + center_sq - 2.0 * cross


def send_kernel(features, a_ref, b_ref, coefs_ref, others_ref, out_ref):
    all_rows, width = a_ref.shape
    rows, pieces = coefs_ref.shape[0], coefs_ref.shape[1] // width
    out_ref[:all_rows, :] = jnp.exp(-(a_ref[...] + b_ref[...]) / features).astype(BF16)
    core = lax.axis_index("feat") % 2
    for half, ref in ((core, coefs_ref), (1 - core, others_ref)):
        for i in range(pieces):
            at = pl.multiple_of(all_rows + (half * pieces + i) * rows, rows)
            out_ref[pl.ds(at, rows), :] = ref[:, i * width : (i + 1) * width]


def product_kernel(sources, rows, scale, *refs):
    tiles, (out_ref, kernel, coefs) = refs[: len(sources)], refs[len(sources) :]
    all_rows, width = kernel.shape[0], tiles[0].shape[1]
    pieces = coefs.shape[1] // width
    core = lax.axis_index("feat") % 2
    for i, (bits, tile) in enumerate(zip(sources, tiles)):
        kernel[:, i * width : (i + 1) * width] = tile[:all_rows, :]
        at = place(bits, rows)
        for j in range(pieces):
            top = pl.multiple_of(all_rows + (core * pieces + j) * rows, rows)
            coefs[pl.ds(at, rows), j * width : (j + 1) * width] = tile[pl.ds(top, rows), :]
    fitted = lax.dot_general(
        coefs[...].T, kernel[...], (((1,), (0,)), ((), ())), preferred_element_type=F32
    ).astype(BF16)
    own = kernel[pl.ds(place((0, 0), rows), rows), :]
    out_ref[...] = scale * lax.dot_general(
        own, fitted, (((1,), (1,)), ((), ())), preferred_element_type=F32
    )


def swap(x, bits):
    return lax.ppermute(x, "feat", [(f, f ^ bits) for f in range(lax.axis_size("feat"))])


def swap_by_core(x, even, odd):
    feats, blks = lax.axis_size("feat"), lax.axis_size("blk")
    pairs = [
        (b * feats + f, (b ^ (odd if f % 2 else even)) * feats + f)
        for b in range(blks)
        for f in range(feats)
    ]
    return lax.ppermute(x, ("blk", "feat"), pairs)


def gather(x, steps):
    held, sources = [x], [(0, 0)]
    for at, even, odd in steps:
        held.append(swap_by_core(held[at], even, odd))
        sources.append((sources[at][0] ^ even, sources[at][1] ^ odd))
    return held, sources


def on_device(points, centers, coefs):
    blks, feats = lax.axis_size("blk"), lax.axis_size("feat")
    rows, local_points = centers.shape[0], points.shape[0]
    all_rows = rows * blks
    features = points.shape[1] * feats

    tiles, sources = gather(centers, GATHER)
    points, tiles[0], square = pl.pallas_call(
        prepare_kernel,
        out_shape=[pltpu.VMEM(points.shape, BF16), pltpu.VMEM(centers.shape, BF16), pltpu.VMEM((1, local_points), F32)],
        in_specs=[VMEM] * 2,
        out_specs=[VMEM] * 3,
        cost_estimate=pl.CostEstimate(flops=2 * points.size, bytes_accessed=2 * points.size, transcendentals=0),
    )(points, centers)
    others = swap(coefs, 1)
    (part,) = call(
        lambda *r: dist_kernel(sources, *r),
        [((all_rows, local_points), F32)],
        points,
        square,
        *tiles,
        scratch=[pltpu.VMEM((all_rows, points.shape[1]), BF16)],
    )
    bits = 1
    while 2 * bits < feats:
        part = part + swap(part, bits)
        bits *= 2
    far = swap(part, bits)
    (tile,) = call(
        lambda *r: send_kernel(float(features), *r),
        [((all_rows + 2 * rows * (coefs.shape[1] // local_points), local_points), BF16)],
        part,
        far,
        coefs,
        others,
    )
    held, sources = gather(tile, SPREAD)
    passed = [i for i, (even, odd) in enumerate(sources) if even != odd]
    held += [swap(held[i], 1) for i in passed]
    sources += [sources[i][::-1] for i in passed]
    scale = 1.0 / math.sqrt(local_points * blks)
    (out,) = call(
        lambda *r: product_kernel(sources, rows, scale, *r),
        [((rows, coefs.shape[1]), F32)],
        *held,
        scratch=[pltpu.VMEM((all_rows, local_points * blks), BF16), pltpu.VMEM((all_rows, coefs.shape[1]), BF16)],
    )
    return out


def on_device_unplanned(points, centers, coefs):
    features = points.shape[1] * lax.axis_size("feat")
    point_sq = jnp.einsum("nf,nf->n", points, points, preferred_element_type=F32)
    center_piece = lax.all_gather(centers, "blk", axis=0, tiled=True)
    center_sq = jnp.einsum("mf,mf->m", center_piece, center_piece, preferred_element_type=F32)
    cross_dot = lax.dot_general(
        points, center_piece, (((1,), (1,)), ((), ())), preferred_element_type=F32
    )
    dist_tile = point_sq[:, None] + center_sq[None, :] - 2.0 * cross_dot
    all_coefs = lax.all_gather(coefs, "blk", axis=0, tiled=True)
    dist = lax.psum(dist_tile, "feat")
    kernel = jnp.exp(-dist / features).astype(BF16)
    fitted = jnp.dot(kernel, all_coefs, preferred_element_type=F32).astype(BF16)
    summed = lax.psum_scatter(
        lax.dot_general(kernel, fitted, (((0,), (0,)), ((), ())), preferred_element_type=F32),
        "blk",
        scatter_dimension=0,
        tiled=True,
    )
    return summed * (1.0 / math.sqrt(points.shape[0] * lax.axis_size("blk")))


def solution(mesh):
    blks, feats = mesh.shape["blk"], mesh.shape["feat"]
    planned = blks == len(GATHER) + 1 and feats % 2 == 0 and feats & (feats - 1) == 0
    return jax.shard_map(
        on_device if planned else on_device_unplanned,
        mesh=mesh,
        in_specs=(P("blk", "feat"),) * 3,
        out_specs=P("blk", "feat"),
        check_vma=False,
    )
```

```python
import math

import jax
import jax.numpy as jnp
from jax import lax
from jax.experimental import pallas as pl
from jax.experimental.pallas import tpu as pltpu
from jax.sharding import PartitionSpec as P

BF16 = jnp.bfloat16
F32 = jnp.float32
VMEM = pl.BlockSpec(memory_space=pltpu.VMEM)

GATHER = ((0, 2, 5), (0, 1, 2), (0, 4, 1), (2, 2, 1), (0, 6, 6), (2, 4, 6), (5, 1, 1))
LATE = (6, 7)
SPREAD = ((0, 4, 5), (0, 6, 7), (0, 2, 3), (0, 1, 1))


def near(x):
    return pltpu.with_memory_space_constraint(x, pltpu.VMEM)


def call(kernel, outs, *args, scratch=()):
    return pl.pallas_call(
        kernel,
        out_shape=[pltpu.VMEM(*o) for o in outs],
        in_specs=[VMEM] * len(args),
        out_specs=[VMEM] * len(outs),
        scratch_shapes=list(scratch),
    )(*[near(x) for x in args])


def place(bits, rows):
    even, odd = bits
    core = lax.axis_index("feat") % 2
    return pl.multiple_of((lax.axis_index("blk") ^ jnp.where(core == 0, even, odd)) * rows, rows)


def prepare_kernel(points_ref, centers_ref, points_out, centers_out, square_out):
    points_out[...] = points_ref[...]
    centers_out[...] = centers_ref[...]
    wide = points_ref[...].astype(F32)
    square_out[...] = jnp.sum((wide * wide).T, axis=0, keepdims=True)


def part_of_dist(centers, points, square):
    cross = lax.dot_general(centers, points, (((1,), (1,)), ((), ())), preferred_element_type=F32)
    wide = centers.astype(F32)
    return square + jnp.sum(wide * wide, axis=1, keepdims=True) - 2.0 * cross


def early_kernel(points_ref, square_ref, *refs):
    tiles, out_ref = refs[:-1], refs[-1]
    centers = jnp.concatenate([tile[...] for tile in tiles], axis=0)
    out_ref[...] = part_of_dist(centers, points_ref[...], square_ref[...])


def dist_kernel(early, late, rows, points_ref, square_ref, early_ref, *refs):
    tiles, part_ref = refs[:-1], refs[-1]
    for i, bits in enumerate(early):
        part_ref[pl.ds(place(bits, rows), rows), :] = early_ref[i * rows : (i + 1) * rows, :]
    centers = jnp.concatenate([tile[...] for tile in tiles], axis=0)
    part = part_of_dist(centers, points_ref[...], square_ref[...])
    for i, bits in enumerate(late):
        part_ref[pl.ds(place(bits, rows), rows), :] = part[i * rows : (i + 1) * rows]


def send_kernel(features, a_ref, b_ref, coefs_ref, others_ref, out_ref):
    all_rows, width = a_ref.shape
    rows, pieces = coefs_ref.shape[0], coefs_ref.shape[1] // width
    out_ref[:all_rows, :] = jnp.exp(-(a_ref[...] + b_ref[...]) / features).astype(BF16)
    core = lax.axis_index("feat") % 2
    for half, ref in ((core, coefs_ref), (1 - core, others_ref)):
        for i in range(pieces):
            at = pl.multiple_of(all_rows + (half * pieces + i) * rows, rows)
            out_ref[pl.ds(at, rows), :] = ref[:, i * width : (i + 1) * width]


def product_kernel(sources, rows, scale, *refs):
    tiles, (out_ref, kernel, coefs) = refs[: len(sources)], refs[len(sources) :]
    all_rows, width = kernel.shape[0], tiles[0].shape[1]
    pieces = coefs.shape[1] // width
    core = lax.axis_index("feat") % 2
    for i, (bits, tile) in enumerate(zip(sources, tiles)):
        kernel[:, i * width : (i + 1) * width] = tile[:all_rows, :]
        at = place(bits, rows)
        for j in range(pieces):
            top = pl.multiple_of(all_rows + (core * pieces + j) * rows, rows)
            coefs[pl.ds(at, rows), j * width : (j + 1) * width] = tile[pl.ds(top, rows), :]
    fitted = lax.dot_general(
        coefs[...].T, kernel[...], (((1,), (0,)), ((), ())), preferred_element_type=F32
    ).astype(BF16)
    own = kernel[pl.ds(place((0, 0), rows), rows), :]
    out_ref[...] = scale * lax.dot_general(
        own, fitted, (((1,), (1,)), ((), ())), preferred_element_type=F32
    )


def swap(x, bits):
    return lax.ppermute(x, "feat", [(f, f ^ bits) for f in range(lax.axis_size("feat"))])


def swap_by_core(x, even, odd):
    feats, blks = lax.axis_size("feat"), lax.axis_size("blk")
    pairs = [
        (b * feats + f, (b ^ (odd if f % 2 else even)) * feats + f)
        for b in range(blks)
        for f in range(feats)
    ]
    return lax.ppermute(x, ("blk", "feat"), pairs)


def gather(x, steps):
    held, sources = [x], [(0, 0)]
    for at, even, odd in steps:
        held.append(swap_by_core(held[at], even, odd))
        sources.append((sources[at][0] ^ even, sources[at][1] ^ odd))
    return held, sources


def on_device(points, centers, coefs):
    blks, feats = lax.axis_size("blk"), lax.axis_size("feat")
    rows, local_points = centers.shape[0], points.shape[0]
    all_rows = rows * blks
    features = points.shape[1] * feats

    tiles, sources = gather(centers, GATHER)
    points, tiles[0], square = pl.pallas_call(
        prepare_kernel,
        out_shape=[pltpu.VMEM(points.shape, BF16), pltpu.VMEM(centers.shape, BF16), pltpu.VMEM((1, local_points), F32)],
        in_specs=[VMEM] * 2,
        out_specs=[VMEM] * 3,
        cost_estimate=pl.CostEstimate(flops=2 * points.size, bytes_accessed=2 * points.size, transcendentals=0),
    )(points, centers)
    others = swap(coefs, 1)
    first = [i for i in range(len(tiles)) if i not in LATE]
    (early,) = call(
        early_kernel,
        [((rows * len(first), local_points), F32)],
        points,
        square,
        *[tiles[i] for i in first],
    )
    (part,) = call(
        lambda *r: dist_kernel([sources[i] for i in first], [sources[i] for i in LATE], rows, *r),
        [((all_rows, local_points), F32)],
        points,
        square,
        early,
        *[tiles[i] for i in LATE],
    )
    bits = 1
    while 2 * bits < feats:
        part = part + swap(part, bits)
        bits *= 2
    far = swap(part, bits)
    (tile,) = call(
        lambda *r: send_kernel(float(features), *r),
        [((all_rows + 2 * rows * (coefs.shape[1] // local_points), local_points), BF16)],
        part,
        far,
        coefs,
        others,
    )
    held, sources = gather(tile, SPREAD)
    passed = [i for i, (even, odd) in enumerate(sources) if even != odd]
    held += [swap(held[i], 1) for i in passed]
    sources += [sources[i][::-1] for i in passed]
    scale = 1.0 / math.sqrt(local_points * blks)
    (out,) = call(
        lambda *r: product_kernel(sources, rows, scale, *r),
        [((rows, coefs.shape[1]), F32)],
        *held,
        scratch=[pltpu.VMEM((all_rows, local_points * blks), BF16), pltpu.VMEM((all_rows, coefs.shape[1]), BF16)],
    )
    return out


def on_device_unplanned(points, centers, coefs):
    features = points.shape[1] * lax.axis_size("feat")
    point_sq = jnp.einsum("nf,nf->n", points, points, preferred_element_type=F32)
    center_piece = lax.all_gather(centers, "blk", axis=0, tiled=True)
    center_sq = jnp.einsum("mf,mf->m", center_piece, center_piece, preferred_element_type=F32)
    cross_dot = lax.dot_general(
        points, center_piece, (((1,), (1,)), ((), ())), preferred_element_type=F32
    )
    dist_tile = point_sq[:, None] + center_sq[None, :] - 2.0 * cross_dot
    all_coefs = lax.all_gather(coefs, "blk", axis=0, tiled=True)
    dist = lax.psum(dist_tile, "feat")
    kernel = jnp.exp(-dist / features).astype(BF16)
    fitted = jnp.dot(kernel, all_coefs, preferred_element_type=F32).astype(BF16)
    summed = lax.psum_scatter(
        lax.dot_general(kernel, fitted, (((0,), (0,)), ((), ())), preferred_element_type=F32),
        "blk",
        scatter_dimension=0,
        tiled=True,
    )
    return summed * (1.0 / math.sqrt(points.shape[0] * lax.axis_size("blk")))


def solution(mesh):
    blks, feats = mesh.shape["blk"], mesh.shape["feat"]
    planned = blks == len(GATHER) + 1 and feats % 2 == 0 and feats & (feats - 1) == 0
    return jax.shard_map(
        on_device if planned else on_device_unplanned,
        mesh=mesh,
        in_specs=(P("blk", "feat"),) * 3,
        out_specs=P("blk", "feat"),
        check_vma=False,
    )
```

```python
import math

import jax
import jax.numpy as jnp
from jax import lax
from jax.experimental import pallas as pl
from jax.experimental.pallas import tpu as pltpu
from jax.sharding import PartitionSpec as P

BF16 = jnp.bfloat16
F32 = jnp.float32
VMEM = pl.BlockSpec(memory_space=pltpu.VMEM)

GATHER = ((0, 2, 5), (0, 1, 2), (0, 4, 1), (2, 2, 1), (0, 6, 6), (2, 4, 6), (5, 1, 1))
LATE = (6, 7)
SPREAD = ((0, 3, 5), (0, 1, 7), (0, 2, 2), (0, 4, 6))


def near(x):
    return pltpu.with_memory_space_constraint(x, pltpu.VMEM)


def call(kernel, outs, *args, scratch=()):
    return pl.pallas_call(
        kernel,
        out_shape=[pltpu.VMEM(*o) for o in outs],
        in_specs=[VMEM] * len(args),
        out_specs=[VMEM] * len(outs),
        scratch_shapes=list(scratch),
    )(*[near(x) for x in args])


def place(bits, rows):
    even, odd = bits
    core = lax.axis_index("feat") % 2
    return pl.multiple_of((lax.axis_index("blk") ^ jnp.where(core == 0, even, odd)) * rows, rows)


def prepare_kernel(points_ref, centers_ref, points_out, centers_out, square_out):
    points_out[...] = points_ref[...]
    centers_out[...] = centers_ref[...]
    wide = points_ref[...].astype(F32)
    square_out[...] = jnp.sum((wide * wide).T, axis=0, keepdims=True)


def part_of_dist(centers, points, square):
    cross = lax.dot_general(centers, points, (((1,), (1,)), ((), ())), preferred_element_type=F32)
    wide = centers.astype(F32)
    return square + jnp.sum(wide * wide, axis=1, keepdims=True) - 2.0 * cross


def early_kernel(points_ref, square_ref, *refs):
    tiles, out_ref = refs[:-1], refs[-1]
    centers = jnp.concatenate([tile[...] for tile in tiles], axis=0)
    out_ref[...] = part_of_dist(centers, points_ref[...], square_ref[...])


def dist_kernel(early, late, rows, points_ref, square_ref, early_ref, *refs):
    tiles, part_ref = refs[:-1], refs[-1]
    for i, bits in enumerate(early):
        part_ref[pl.ds(place(bits, rows), rows), :] = early_ref[i * rows : (i + 1) * rows, :]
    centers = jnp.concatenate([tile[...] for tile in tiles], axis=0)
    part = part_of_dist(centers, points_ref[...], square_ref[...])
    for i, bits in enumerate(late):
        part_ref[pl.ds(place(bits, rows), rows), :] = part[i * rows : (i + 1) * rows]


def send_kernel(features, a_ref, b_ref, coefs_ref, others_ref, out_ref):
    all_rows, width = a_ref.shape
    rows, pieces = coefs_ref.shape[0], coefs_ref.shape[1] // width
    out_ref[:all_rows, :] = jnp.exp(-(a_ref[...] + b_ref[...]) / features).astype(BF16)
    core = lax.axis_index("feat") % 2
    for half, ref in ((core, coefs_ref), (1 - core, others_ref)):
        for i in range(pieces):
            at = pl.multiple_of(all_rows + (half * pieces + i) * rows, rows)
            out_ref[pl.ds(at, rows), :] = ref[:, i * width : (i + 1) * width]


def product_kernel(sources, rows, scale, *refs):
    tiles, (out_ref, kernel, coefs) = refs[: len(sources)], refs[len(sources) :]
    all_rows, width = kernel.shape[0], tiles[0].shape[1]
    pieces = coefs.shape[1] // width
    core = lax.axis_index("feat") % 2
    for i, (bits, tile) in enumerate(zip(sources, tiles)):
        kernel[:, i * width : (i + 1) * width] = tile[:all_rows, :]
        at = place(bits, rows)
        for j in range(pieces):
            top = pl.multiple_of(all_rows + (core * pieces + j) * rows, rows)
            coefs[pl.ds(at, rows), j * width : (j + 1) * width] = tile[pl.ds(top, rows), :]
    fitted = lax.dot_general(
        coefs[...].T, kernel[...], (((1,), (0,)), ((), ())), preferred_element_type=F32
    ).astype(BF16)
    own = kernel[pl.ds(place((0, 0), rows), rows), :]
    out_ref[...] = scale * lax.dot_general(
        own, fitted, (((1,), (1,)), ((), ())), preferred_element_type=F32
    )


def swap(x, bits):
    return lax.ppermute(x, "feat", [(f, f ^ bits) for f in range(lax.axis_size("feat"))])


def swap_by_core(x, even, odd):
    feats, blks = lax.axis_size("feat"), lax.axis_size("blk")
    pairs = [
        (b * feats + f, (b ^ (odd if f % 2 else even)) * feats + f)
        for b in range(blks)
        for f in range(feats)
    ]
    return lax.ppermute(x, ("blk", "feat"), pairs)


def gather(x, steps):
    held, sources = [x], [(0, 0)]
    for at, even, odd in steps:
        held.append(swap_by_core(held[at], even, odd))
        sources.append((sources[at][0] ^ even, sources[at][1] ^ odd))
    return held, sources


def on_device(points, centers, coefs):
    blks, feats = lax.axis_size("blk"), lax.axis_size("feat")
    rows, local_points = centers.shape[0], points.shape[0]
    all_rows = rows * blks
    features = points.shape[1] * feats

    tiles, sources = gather(centers, GATHER)
    points, tiles[0], square = pl.pallas_call(
        prepare_kernel,
        out_shape=[pltpu.VMEM(points.shape, BF16), pltpu.VMEM(centers.shape, BF16), pltpu.VMEM((1, local_points), F32)],
        in_specs=[VMEM] * 2,
        out_specs=[VMEM] * 3,
        cost_estimate=pl.CostEstimate(flops=2 * points.size, bytes_accessed=2 * points.size, transcendentals=0),
    )(points, centers)
    others = swap(coefs, 1)
    first = [i for i in range(len(tiles)) if i not in LATE]
    (early,) = call(
        early_kernel,
        [((rows * len(first), local_points), F32)],
        points,
        square,
        *[tiles[i] for i in first],
    )
    (part,) = call(
        lambda *r: dist_kernel([sources[i] for i in first], [sources[i] for i in LATE], rows, *r),
        [((all_rows, local_points), F32)],
        points,
        square,
        early,
        *[tiles[i] for i in LATE],
    )
    bits = 1
    while 2 * bits < feats:
        part = part + swap(part, bits)
        bits *= 2
    far = swap(part, bits)
    (tile,) = call(
        lambda *r: send_kernel(float(features), *r),
        [((all_rows + 2 * rows * (coefs.shape[1] // local_points), local_points), BF16)],
        part,
        far,
        coefs,
        others,
    )
    held, sources = gather(tile, SPREAD)
    passed = [i for i, (even, odd) in enumerate(sources) if even != odd]
    held += [swap(held[i], 1) for i in passed]
    sources += [sources[i][::-1] for i in passed]
    scale = 1.0 / math.sqrt(local_points * blks)
    (out,) = call(
        lambda *r: product_kernel(sources, rows, scale, *r),
        [((rows, coefs.shape[1]), F32)],
        *held,
        scratch=[pltpu.VMEM((all_rows, local_points * blks), BF16), pltpu.VMEM((all_rows, coefs.shape[1]), BF16)],
    )
    return out


def on_device_unplanned(points, centers, coefs):
    features = points.shape[1] * lax.axis_size("feat")
    point_sq = jnp.einsum("nf,nf->n", points, points, preferred_element_type=F32)
    center_piece = lax.all_gather(centers, "blk", axis=0, tiled=True)
    center_sq = jnp.einsum("mf,mf->m", center_piece, center_piece, preferred_element_type=F32)
    cross_dot = lax.dot_general(
        points, center_piece, (((1,), (1,)), ((), ())), preferred_element_type=F32
    )
    dist_tile = point_sq[:, None] + center_sq[None, :] - 2.0 * cross_dot
    all_coefs = lax.all_gather(coefs, "blk", axis=0, tiled=True)
    dist = lax.psum(dist_tile, "feat")
    kernel = jnp.exp(-dist / features).astype(BF16)
    fitted = jnp.dot(kernel, all_coefs, preferred_element_type=F32).astype(BF16)
    summed = lax.psum_scatter(
        lax.dot_general(kernel, fitted, (((0,), (0,)), ((), ())), preferred_element_type=F32),
        "blk",
        scatter_dimension=0,
        tiled=True,
    )
    return summed * (1.0 / math.sqrt(points.shape[0] * lax.axis_size("blk")))


def solution(mesh):
    blks, feats = mesh.shape["blk"], mesh.shape["feat"]
    planned = blks == len(GATHER) + 1 and feats % 2 == 0 and feats & (feats - 1) == 0
    return jax.shard_map(
        on_device if planned else on_device_unplanned,
        mesh=mesh,
        in_specs=(P("blk", "feat"),) * 3,
        out_specs=P("blk", "feat"),
        check_vma=False,
    )
```

```python
import math

import jax
import jax.numpy as jnp
from jax import lax
from jax.experimental import pallas as pl
from jax.experimental.pallas import tpu as pltpu
from jax.sharding import PartitionSpec as P

BF16 = jnp.bfloat16
F32 = jnp.float32
VMEM = pl.BlockSpec(memory_space=pltpu.VMEM)

GATHER = ((0, 2, 5), (0, 1, 2), (0, 4, 1), (2, 2, 1), (0, 6, 6), (2, 4, 6), (5, 1, 1))
LATE = (7,)
SPREAD = ((0, 3, 5), (0, 1, 7), (0, 2, 2), (0, 4, 6))


def near(x):
    return pltpu.with_memory_space_constraint(x, pltpu.VMEM)


def call(kernel, outs, *args, scratch=()):
    return pl.pallas_call(
        kernel,
        out_shape=[pltpu.VMEM(*o) for o in outs],
        in_specs=[VMEM] * len(args),
        out_specs=[VMEM] * len(outs),
        scratch_shapes=list(scratch),
    )(*[near(x) for x in args])


def place(bits, rows):
    even, odd = bits
    core = lax.axis_index("feat") % 2
    return pl.multiple_of((lax.axis_index("blk") ^ jnp.where(core == 0, even, odd)) * rows, rows)


def prepare_kernel(points_ref, centers_ref, points_out, centers_out, square_out):
    points_out[...] = points_ref[...]
    centers_out[...] = centers_ref[...]
    wide = points_ref[...].astype(F32)
    square_out[...] = jnp.sum((wide * wide).T, axis=0, keepdims=True)


def part_of_dist(centers, points, square):
    cross = lax.dot_general(centers, points, (((1,), (1,)), ((), ())), preferred_element_type=F32)
    wide = centers.astype(F32)
    return square + jnp.sum(wide * wide, axis=1, keepdims=True) - 2.0 * cross


def early_kernel(points_ref, square_ref, *refs):
    tiles, out_ref = refs[:-1], refs[-1]
    centers = jnp.concatenate([tile[...] for tile in tiles], axis=0)
    out_ref[...] = part_of_dist(centers, points_ref[...], square_ref[...])


def dist_kernel(early, late, rows, points_ref, square_ref, early_ref, *refs):
    tiles, part_ref = refs[:-1], refs[-1]
    for i, bits in enumerate(early):
        part_ref[pl.ds(place(bits, rows), rows), :] = early_ref[i * rows : (i + 1) * rows, :]
    centers = jnp.concatenate([tile[...] for tile in tiles], axis=0)
    part = part_of_dist(centers, points_ref[...], square_ref[...])
    for i, bits in enumerate(late):
        part_ref[pl.ds(place(bits, rows), rows), :] = part[i * rows : (i + 1) * rows]


def send_kernel(features, a_ref, b_ref, coefs_ref, others_ref, out_ref):
    all_rows, width = a_ref.shape
    rows, pieces = coefs_ref.shape[0], coefs_ref.shape[1] // width
    out_ref[:all_rows, :] = jnp.exp(-(a_ref[...] + b_ref[...]) / features).astype(BF16)
    core = lax.axis_index("feat") % 2
    for half, ref in ((core, coefs_ref), (1 - core, others_ref)):
        for i in range(pieces):
            at = pl.multiple_of(all_rows + (half * pieces + i) * rows, rows)
            out_ref[pl.ds(at, rows), :] = ref[:, i * width : (i + 1) * width]


def product_kernel(sources, rows, scale, *refs):
    tiles, (out_ref, kernel, coefs) = refs[: len(sources)], refs[len(sources) :]
    all_rows, width = kernel.shape[0], tiles[0].shape[1]
    pieces = coefs.shape[1] // width
    core = lax.axis_index("feat") % 2
    for i, (bits, tile) in enumerate(zip(sources, tiles)):
        kernel[:, i * width : (i + 1) * width] = tile[:all_rows, :]
        at = place(bits, rows)
        for j in range(pieces):
            top = pl.multiple_of(all_rows + (core * pieces + j) * rows, rows)
            coefs[pl.ds(at, rows), j * width : (j + 1) * width] = tile[pl.ds(top, rows), :]
    fitted = lax.dot_general(
        coefs[...].T, kernel[...], (((1,), (0,)), ((), ())), preferred_element_type=F32
    ).astype(BF16)
    own = kernel[pl.ds(place((0, 0), rows), rows), :]
    out_ref[...] = scale * lax.dot_general(
        own, fitted, (((1,), (1,)), ((), ())), preferred_element_type=F32
    )


def swap(x, bits):
    return lax.ppermute(x, "feat", [(f, f ^ bits) for f in range(lax.axis_size("feat"))])


def swap_by_core(x, even, odd):
    feats, blks = lax.axis_size("feat"), lax.axis_size("blk")
    pairs = [
        (b * feats + f, (b ^ (odd if f % 2 else even)) * feats + f)
        for b in range(blks)
        for f in range(feats)
    ]
    return lax.ppermute(x, ("blk", "feat"), pairs)


def gather(x, steps):
    held, sources = [x], [(0, 0)]
    for at, even, odd in steps:
        held.append(swap_by_core(held[at], even, odd))
        sources.append((sources[at][0] ^ even, sources[at][1] ^ odd))
    return held, sources


def on_device(points, centers, coefs):
    blks, feats = lax.axis_size("blk"), lax.axis_size("feat")
    rows, local_points = centers.shape[0], points.shape[0]
    all_rows = rows * blks
    features = points.shape[1] * feats

    tiles, sources = gather(centers, GATHER)
    points, tiles[0], square = pl.pallas_call(
        prepare_kernel,
        out_shape=[pltpu.VMEM(points.shape, BF16), pltpu.VMEM(centers.shape, BF16), pltpu.VMEM((1, local_points), F32)],
        in_specs=[VMEM] * 2,
        out_specs=[VMEM] * 3,
        cost_estimate=pl.CostEstimate(flops=2 * points.size, bytes_accessed=2 * points.size, transcendentals=0),
    )(points, centers)
    others = swap(coefs, 1)
    first = [i for i in range(len(tiles)) if i not in LATE]
    (early,) = call(
        early_kernel,
        [((rows * len(first), local_points), F32)],
        points,
        square,
        *[tiles[i] for i in first],
    )
    (part,) = call(
        lambda *r: dist_kernel([sources[i] for i in first], [sources[i] for i in LATE], rows, *r),
        [((all_rows, local_points), F32)],
        points,
        square,
        early,
        *[tiles[i] for i in LATE],
    )
    bits = 1
    while 2 * bits < feats:
        part = part + swap(part, bits)
        bits *= 2
    far = swap(part, bits)
    (tile,) = call(
        lambda *r: send_kernel(float(features), *r),
        [((all_rows + 2 * rows * (coefs.shape[1] // local_points), local_points), BF16)],
        part,
        far,
        coefs,
        others,
    )
    held, sources = gather(tile, SPREAD)
    passed = [i for i, (even, odd) in enumerate(sources) if even != odd]
    held += [swap(held[i], 1) for i in passed]
    sources += [sources[i][::-1] for i in passed]
    scale = 1.0 / math.sqrt(local_points * blks)
    (out,) = call(
        lambda *r: product_kernel(sources, rows, scale, *r),
        [((rows, coefs.shape[1]), F32)],
        *held,
        scratch=[pltpu.VMEM((all_rows, local_points * blks), BF16), pltpu.VMEM((all_rows, coefs.shape[1]), BF16)],
    )
    return out


def on_device_unplanned(points, centers, coefs):
    features = points.shape[1] * lax.axis_size("feat")
    point_sq = jnp.einsum("nf,nf->n", points, points, preferred_element_type=F32)
    center_piece = lax.all_gather(centers, "blk", axis=0, tiled=True)
    center_sq = jnp.einsum("mf,mf->m", center_piece, center_piece, preferred_element_type=F32)
    cross_dot = lax.dot_general(
        points, center_piece, (((1,), (1,)), ((), ())), preferred_element_type=F32
    )
    dist_tile = point_sq[:, None] + center_sq[None, :] - 2.0 * cross_dot
    all_coefs = lax.all_gather(coefs, "blk", axis=0, tiled=True)
    dist = lax.psum(dist_tile, "feat")
    kernel = jnp.exp(-dist / features).astype(BF16)
    fitted = jnp.dot(kernel, all_coefs, preferred_element_type=F32).astype(BF16)
    summed = lax.psum_scatter(
        lax.dot_general(kernel, fitted, (((0,), (0,)), ((), ())), preferred_element_type=F32),
        "blk",
        scatter_dimension=0,
        tiled=True,
    )
    return summed * (1.0 / math.sqrt(points.shape[0] * lax.axis_size("blk")))


def solution(mesh):
    blks, feats = mesh.shape["blk"], mesh.shape["feat"]
    planned = blks == len(GATHER) + 1 and feats % 2 == 0 and feats & (feats - 1) == 0
    return jax.shard_map(
        on_device if planned else on_device_unplanned,
        mesh=mesh,
        in_specs=(P("blk", "feat"),) * 3,
        out_specs=P("blk", "feat"),
        check_vma=False,
    )
```

```python
import math

import jax
import jax.numpy as jnp
from jax import lax
from jax.experimental import pallas as pl
from jax.experimental.pallas import tpu as pltpu
from jax.sharding import PartitionSpec as P

BF16 = jnp.bfloat16
F32 = jnp.float32
VMEM = pl.BlockSpec(memory_space=pltpu.VMEM)

GATHER = ((0, 1, 2), (0, 2, 1), (1, 2, 1), (0, 4, 5), (0, 6, 6), (1, 4, 6), (5, 1, 1))
LATE = (7,)
SPREAD = ((0, 3, 5), (0, 1, 7), (0, 2, 2), (0, 4, 6))


def near(x):
    return pltpu.with_memory_space_constraint(x, pltpu.VMEM)


def call(kernel, outs, *args, scratch=()):
    return pl.pallas_call(
        kernel,
        out_shape=[pltpu.VMEM(*o) for o in outs],
        in_specs=[VMEM] * len(args),
        out_specs=[VMEM] * len(outs),
        scratch_shapes=list(scratch),
    )(*[near(x) for x in args])


def place(bits, rows):
    even, odd = bits
    core = lax.axis_index("feat") % 2
    return pl.multiple_of((lax.axis_index("blk") ^ jnp.where(core == 0, even, odd)) * rows, rows)


def prepare_kernel(points_ref, centers_ref, points_out, centers_out, square_out):
    points_out[...] = points_ref[...]
    centers_out[...] = centers_ref[...]
    wide = points_ref[...].astype(F32)
    square_out[...] = jnp.sum((wide * wide).T, axis=0, keepdims=True)


def part_of_dist(centers, points, square):
    cross = lax.dot_general(centers, points, (((1,), (1,)), ((), ())), preferred_element_type=F32)
    wide = centers.astype(F32)
    return square + jnp.sum(wide * wide, axis=1, keepdims=True) - 2.0 * cross


def early_kernel(points_ref, square_ref, *refs):
    tiles, out_ref = refs[:-1], refs[-1]
    centers = jnp.concatenate([tile[...] for tile in tiles], axis=0)
    out_ref[...] = part_of_dist(centers, points_ref[...], square_ref[...])


def dist_kernel(early, late, rows, points_ref, square_ref, early_ref, *refs):
    tiles, part_ref = refs[:-1], refs[-1]
    for i, bits in enumerate(early):
        part_ref[pl.ds(place(bits, rows), rows), :] = early_ref[i * rows : (i + 1) * rows, :]
    centers = jnp.concatenate([tile[...] for tile in tiles], axis=0)
    part = part_of_dist(centers, points_ref[...], square_ref[...])
    for i, bits in enumerate(late):
        part_ref[pl.ds(place(bits, rows), rows), :] = part[i * rows : (i + 1) * rows]


def send_kernel(features, a_ref, b_ref, coefs_ref, others_ref, out_ref):
    all_rows, width = a_ref.shape
    rows, pieces = coefs_ref.shape[0], coefs_ref.shape[1] // width
    out_ref[:all_rows, :] = jnp.exp(-(a_ref[...] + b_ref[...]) / features).astype(BF16)
    core = lax.axis_index("feat") % 2
    for half, ref in ((core, coefs_ref), (1 - core, others_ref)):
        for i in range(pieces):
            at = pl.multiple_of(all_rows + (half * pieces + i) * rows, rows)
            out_ref[pl.ds(at, rows), :] = ref[:, i * width : (i + 1) * width]


def product_kernel(sources, rows, scale, *refs):
    tiles, (out_ref, kernel, coefs) = refs[: len(sources)], refs[len(sources) :]
    all_rows, width = kernel.shape[0], tiles[0].shape[1]
    pieces = coefs.shape[1] // width
    core = lax.axis_index("feat") % 2
    for i, (bits, tile) in enumerate(zip(sources, tiles)):
        kernel[:, i * width : (i + 1) * width] = tile[:all_rows, :]
        at = place(bits, rows)
        for j in range(pieces):
            top = pl.multiple_of(all_rows + (core * pieces + j) * rows, rows)
            coefs[pl.ds(at, rows), j * width : (j + 1) * width] = tile[pl.ds(top, rows), :]
    fitted = lax.dot_general(
        coefs[...].T, kernel[...], (((1,), (0,)), ((), ())), preferred_element_type=F32
    ).astype(BF16)
    own = kernel[pl.ds(place((0, 0), rows), rows), :]
    out_ref[...] = scale * lax.dot_general(
        own, fitted, (((1,), (1,)), ((), ())), preferred_element_type=F32
    )


def swap(x, bits):
    return lax.ppermute(x, "feat", [(f, f ^ bits) for f in range(lax.axis_size("feat"))])


def swap_by_core(x, even, odd):
    feats, blks = lax.axis_size("feat"), lax.axis_size("blk")
    pairs = [
        (b * feats + f, (b ^ (odd if f % 2 else even)) * feats + f)
        for b in range(blks)
        for f in range(feats)
    ]
    return lax.ppermute(x, ("blk", "feat"), pairs)


def gather(x, steps):
    held, sources = [x], [(0, 0)]
    for at, even, odd in steps:
        held.append(swap_by_core(held[at], even, odd))
        sources.append((sources[at][0] ^ even, sources[at][1] ^ odd))
    return held, sources


def on_device(points, centers, coefs):
    blks, feats = lax.axis_size("blk"), lax.axis_size("feat")
    rows, local_points = centers.shape[0], points.shape[0]
    all_rows = rows * blks
    features = points.shape[1] * feats

    tiles, sources = gather(centers, GATHER)
    points, tiles[0], square = pl.pallas_call(
        prepare_kernel,
        out_shape=[pltpu.VMEM(points.shape, BF16), pltpu.VMEM(centers.shape, BF16), pltpu.VMEM((1, local_points), F32)],
        in_specs=[VMEM] * 2,
        out_specs=[VMEM] * 3,
        cost_estimate=pl.CostEstimate(flops=2 * points.size, bytes_accessed=2 * points.size, transcendentals=0),
    )(points, centers)
    others = swap(coefs, 1)
    first = [i for i in range(len(tiles)) if i not in LATE]
    (early,) = call(
        early_kernel,
        [((rows * len(first), local_points), F32)],
        points,
        square,
        *[tiles[i] for i in first],
    )
    (part,) = call(
        lambda *r: dist_kernel([sources[i] for i in first], [sources[i] for i in LATE], rows, *r),
        [((all_rows, local_points), F32)],
        points,
        square,
        early,
        *[tiles[i] for i in LATE],
    )
    bits = 1
    while 2 * bits < feats:
        part = part + swap(part, bits)
        bits *= 2
    far = swap(part, bits)
    (tile,) = call(
        lambda *r: send_kernel(float(features), *r),
        [((all_rows + 2 * rows * (coefs.shape[1] // local_points), local_points), BF16)],
        part,
        far,
        coefs,
        others,
    )
    held, sources = gather(tile, SPREAD)
    passed = [i for i, (even, odd) in enumerate(sources) if even != odd]
    held += [swap(held[i], 1) for i in passed]
    sources += [sources[i][::-1] for i in passed]
    scale = 1.0 / math.sqrt(local_points * blks)
    (out,) = call(
        lambda *r: product_kernel(sources, rows, scale, *r),
        [((rows, coefs.shape[1]), F32)],
        *held,
        scratch=[pltpu.VMEM((all_rows, local_points * blks), BF16), pltpu.VMEM((all_rows, coefs.shape[1]), BF16)],
    )
    return out


def on_device_unplanned(points, centers, coefs):
    features = points.shape[1] * lax.axis_size("feat")
    point_sq = jnp.einsum("nf,nf->n", points, points, preferred_element_type=F32)
    center_piece = lax.all_gather(centers, "blk", axis=0, tiled=True)
    center_sq = jnp.einsum("mf,mf->m", center_piece, center_piece, preferred_element_type=F32)
    cross_dot = lax.dot_general(
        points, center_piece, (((1,), (1,)), ((), ())), preferred_element_type=F32
    )
    dist_tile = point_sq[:, None] + center_sq[None, :] - 2.0 * cross_dot
    all_coefs = lax.all_gather(coefs, "blk", axis=0, tiled=True)
    dist = lax.psum(dist_tile, "feat")
    kernel = jnp.exp(-dist / features).astype(BF16)
    fitted = jnp.dot(kernel, all_coefs, preferred_element_type=F32).astype(BF16)
    summed = lax.psum_scatter(
        lax.dot_general(kernel, fitted, (((0,), (0,)), ((), ())), preferred_element_type=F32),
        "blk",
        scatter_dimension=0,
        tiled=True,
    )
    return summed * (1.0 / math.sqrt(points.shape[0] * lax.axis_size("blk")))


def solution(mesh):
    blks, feats = mesh.shape["blk"], mesh.shape["feat"]
    planned = blks == len(GATHER) + 1 and feats % 2 == 0 and feats & (feats - 1) == 0
    return jax.shard_map(
        on_device if planned else on_device_unplanned,
        mesh=mesh,
        in_specs=(P("blk", "feat"),) * 3,
        out_specs=P("blk", "feat"),
        check_vma=False,
    )
```
